128 devices in a mesh: img: 16 (over y, x), own: 8 (over z, core).
Axes of the slice: x: 4, y: 4, z: 4, core: 2. Of those that a mesh axis runs over, the one named last changes fastest.
Arguments:
- patches: bfloat16 [25088, 4608], P(('img', 'own')), may hold values from -6 to 6
- grads: bfloat16 [25088, 512], P(('img', 'own')), may hold values from -0.8984375 to 0.8984375
- basis_g: bfloat16 [512, 512], replicated, may hold values from -0.25 to 0.25
- basis_slots: bfloat16 [4608, 9216], P(None, 'own'), may hold values from -0.09375 to 0.09375
- col_counts: int32 [8], replicated, may hold values from 1 to 1152, 4608 in all
Outputs:
- corrections: float32 [4608, 512], P(('img', 'own'))
The draws below stay inside these ranges and needn't reach their ends.
Inputs may be any that keep to these rules, and one draw needn't show every extreme that they name: `col_counts`: the counts sum to 4608; one owner has exactly 1152.
All inputs are finite; a program needn't handle non-finite values.
Results may differ from the reference program's by a relative error of at most 0.00049.
Values may be sent and summed in bfloat16 or wider, within the bound.
No kernel may reach another device: no remote copies, remote signals or barrier semaphores. Data moves between devices by JAX's collectives and lax.ppermute only.
A program may use at most 128 MiB of HBM per device.

```python
import math
import jax
import jax.numpy as jnp
import numpy as np
from jax import lax

KIN = 4608
GOUT = 512
POS = 49
IMG_DEV = 4
CAP = 1152
IMAGES = 512
ROWS = 25088
N_OWN = 8


def levels(key, dims, split, smallest, top_value):
    level = 1.0
    for position, shards_of in split:
        heights = jax.random.uniform(jax.random.fold_in(jax.random.fold_in(key, 6), position), (shards_of,), jnp.float32, smallest / len(split), top_value / len(split))
        level = level * jnp.repeat(jnp.exp(heights), dims[position] // shards_of).reshape((-1,) + (1,) * (len(dims) - 1 - position))
    return level


def length_profile(number_of, total, limit, lean):
    weights = [(1 << 20) // math.isqrt(rank ** lean) + 1 for rank in range(2, number_of + 1)]
    surplus, given = total - limit - (number_of - 1), [1] * (number_of - 1)
    while surplus > 0:
        free = [i for i in range(number_of - 1) if given[i] < limit]
        pool, left = sum([weights[i] for i in free]), surplus
        for i in free:
            extra = min(limit - given[i], max(1, left * weights[i] // pool), surplus)
            given[i] = given[i] + extra
            surplus = surplus - extra
    return np.array([limit] + given)


def ragged_sizes(key, count, total, bound, skew):
    if count == 2:
        one = jax.random.randint(key, (), max(1, total - bound), min(bound, total - 1) + 1)
        return jnp.stack([one, total - one])
    lengths = jnp.asarray(length_profile(count, total, bound, skew), jnp.int32)
    pairs = (count - 1) // 2
    giver, receiver = lengths[1:1 + 2 * pairs:2], lengths[2:2 + 2 * pairs:2]
    room = jnp.minimum(giver - 1, bound - receiver)
    passed = jax.random.randint(jax.random.fold_in(key, 1), (pairs,), 0, 1 << 20) % (room + 1)
    lengths = lengths.at[1:1 + 2 * pairs:2].set(giver - passed).at[2:2 + 2 * pairs:2].set(receiver + passed)
    return lengths[jax.random.permutation(jax.random.fold_in(key, 2), count)]


def gaussian(stream_key, dims, width, limit, split=(), held_as=jnp.bfloat16):
    entries = width * jax.random.normal(stream_key, dims, jnp.float32)
    if split:
        entries = entries * levels(stream_key, dims, split, -0.22, 0.18)
    return jnp.clip(entries, -limit, limit).astype(held_as)


def setup_inputs(seed: int = 0) -> dict:
    seeds = jax.random.split(jax.random.key(seed), 6)
    return {
        "patches": gaussian(seeds[0], (ROWS, KIN), 1.0, 6.0, ((0, 128),)),
        "grads": gaussian(seeds[1], (ROWS, GOUT), 0.15, 0.8984375, ((0, 128),)),
        "basis_g": gaussian(seeds[2], (GOUT, GOUT), GOUT ** -0.5, 0.25),
        "basis_slots": gaussian(seeds[3], (KIN, N_OWN * CAP), KIN ** -0.5, 0.09375, ((1, 8),)),
        "col_counts": ragged_sizes(seeds[4], N_OWN, KIN, CAP, 2).astype(jnp.int32),
    }


def reference(patches, grads, basis_g, basis_slots, col_counts):
    block = IMG_DEV
    steps_count = IMAGES // block
    patch_blocks = patches.reshape(steps_count, block * POS, KIN)
    grad_blocks = grads.reshape(steps_count, block * POS, GOUT)

    def accumulate(total, pieces):
        patch_piece, grad_piece = pieces
        proj_g = jnp.dot(grad_piece, basis_g, preferred_element_type=jnp.float32).astype(jnp.bfloat16)
        proj_a = jnp.dot(patch_piece, basis_slots, preferred_element_type=jnp.float32).astype(jnp.bfloat16)
        proj_g = proj_g.reshape(block, POS, GOUT).astype(jnp.float32)
        proj_a = proj_a.reshape(block, POS, N_OWN * CAP).astype(jnp.float32)
        coef = jnp.einsum("nps,npg->nsg", proj_a, proj_g)
        return total + jnp.sum(coef * coef, axis=0), None

    start_total = jnp.zeros((N_OWN * CAP, GOUT), jnp.float32)
    slot_corr, unused = lax.scan(accumulate, start_total, (patch_blocks, grad_blocks))
    slot_corr = slot_corr / jnp.float32(IMAGES)
    counts = col_counts.astype(jnp.int32)
    starts = (jnp.cumsum(counts) - counts).astype(jnp.int32)
    slot_index = jnp.arange(CAP, dtype=jnp.int32)
    result = jnp.zeros((KIN + CAP, GOUT), jnp.float32)
    for owner in range(N_OWN):
        piece = slot_corr[owner * CAP:(owner + 1) * CAP]
        piece = jnp.where((slot_index < counts[owner])[:, None], piece, jnp.float32(0.0))
        placed = lax.dynamic_update_slice(jnp.zeros((KIN + CAP, GOUT), jnp.float32), piece, (starts[owner], jnp.int32(0)))
        result = result + placed
    return result[:KIN]
```

```python
import jax
import jax.numpy as jnp
from jax import lax
from jax.sharding import PartitionSpec as P

POS = 49


def shards(patches, grads, basis_g, basis_slots, col_counts):
    groups = lax.axis_size("img")
    owners = lax.axis_size("own")
    img = lax.axis_index("img")
    own = lax.axis_index("own")
    f32, bf16, i32 = jnp.float32, jnp.bfloat16, jnp.int32
    rows = patches.shape[0]
    kin, cap = basis_slots.shape
    gout = basis_g.shape[1]
    blk = kin // (groups * owners)
    stripe = blk * owners
    ring = -(-cap // stripe) * stripe
    per = ring // owners
    cols = blk * groups
    depth = kin // groups
    starts = jnp.cumsum(col_counts) - col_counts
    my_count = col_counts[own]
    my_start = starts[own]

    proj = jnp.dot(grads, basis_g, preferred_element_type=f32).astype(bf16)
    everything = lax.all_gather(jnp.concatenate([patches, proj], axis=1), "own", axis=0)

    piece = lax.dynamic_slice(basis_slots, (img * depth, jnp.int32(0)), (depth, cap))
    slot = jnp.arange(cap, dtype=i32)
    place = (my_start + slot) % ring
    place = (place % stripe) // blk * per + place // stripe * blk + place % blk
    send = (jnp.arange(ring, dtype=i32)[:, None] == place[None, :]) & (slot < my_count)[None, :]
    outgoing = lax.dot_general(
        send.astype(bf16), piece, (((1,), (1,)), ((), ())), preferred_element_type=f32
    ).astype(bf16)
    incoming = lax.all_to_all(outgoing.reshape(owners, per, depth), "own", 0, 0, tiled=True)
    spot = jnp.arange(per, dtype=i32)
    at = spot // blk * stripe + own * blk + spot % blk
    offset = (at[None, :] - starts[:, None]) % ring
    column = starts[:, None] + offset
    target = jnp.where(offset < col_counts[:, None], column // stripe * blk + column % blk, -1)
    keep = target.reshape(ring)[:, None] == jnp.arange(cols, dtype=i32)[None, :]
    mine = lax.dot_general(
        incoming.reshape(ring, depth), keep.astype(bf16), (((0,), (0,)), ((), ())), preferred_element_type=f32
    ).astype(bf16)
    basis = lax.all_gather(mine, "img", axis=0, tiled=True)

    proj_a = jnp.einsum("drk,kc->drc", everything[:, :, :kin], basis, preferred_element_type=f32).astype(bf16)
    images = owners * rows // POS
    coef = jnp.einsum(
        "nps,npg->nsg",
        proj_a.reshape(images, POS, cols),
        everything[:, :, kin:].reshape(images, POS, gout),
        preferred_element_type=f32,
    )
    total = jnp.sum(coef * coef, axis=0)
    parts = lax.all_to_all(total.reshape(groups, blk, gout), "img", 0, 0, tiled=True)
    return jnp.sum(parts, axis=0) / f32(images * groups)


def solution(mesh):
    in_specs = (P(("img", "own"), None), P(("img", "own"), None), P(), P(None, "own"), P())
    out_specs = P(("img", "own"), None)
    return jax.shard_map(shards, mesh=mesh, in_specs=in_specs, out_specs=out_specs, check_vma=False)
```

```python
import functools

import jax
import jax.numpy as jnp
from jax import lax
from jax.experimental import pallas as pl
from jax.experimental.pallas import tpu as pltpu
from jax.sharding import PartitionSpec as P

POS = 49
CHIPS = 4
CORES = 2
F32, BF16, I32 = jnp.float32, jnp.bfloat16, jnp.int32


def accumulate(n, chunk, *refs):
    lows, highs = refs[:n], refs[n : 2 * n]
    basis, *before, total, low, high, held, flip, sems = refs[2 * n :]
    rows, half = low.shape[1:]
    kin, cols = held.shape
    rest = kin - half
    gout = half - rest
    first = pltpu.make_async_copy(basis.at[pl.ds(0, half)], held.at[pl.ds(0, half)], sems.at[0])
    second = pltpu.make_async_copy(basis.at[pl.ds(half, rest)], held.at[pl.ds(half, rest)], sems.at[1])
    lefts = [pltpu.make_async_copy(lows[k], low.at[k], sems.at[2 + 2 * k]) for k in range(n)]
    rights = [pltpu.make_async_copy(highs[k], high.at[k], sems.at[3 + 2 * k]) for k in range(n)]
    first.start()
    lefts[0].start()
    second.start()
    rights[0].start()
    image = lax.broadcasted_iota(I32, (rows, gout), 0) // POS
    for k in range(n):
        lefts[k].wait()
        if k == 0:
            first.wait()
        if k + 1 < n:
            lefts[k + 1].start()
            rights[k + 1].start()
        proj = jnp.dot(low[k], held[:half], preferred_element_type=F32)
        rights[k].wait()
        if k == 0:
            second.wait()
        proj += jnp.dot(high[k, :, :rest], held[half:], preferred_element_type=F32)
        flip[...] = proj.astype(BF16).T
        grads = high[k, :, rest:]
        apart = [jnp.where(image == m, grads, jnp.zeros_like(grads)) for m in range(rows // POS)]
        for s in range(0, cols, chunk):
            left = flip[s : s + chunk]
            source = (total if k else before[0] if before else None)
            squares = jnp.zeros((chunk, gout), F32) if source is None else source[s : s + chunk]
            for one in apart:
                coef = jnp.dot(left, one, preferred_element_type=F32)
                squares += coef * coef
            total[s : s + chunk] = squares


def added(lows, highs, basis, *before):
    n = len(lows)
    rows, half = lows[0].shape
    kin, cols = basis.shape
    gout = 2 * half - kin
    anywhere = pl.BlockSpec(memory_space=pl.ANY)
    return pl.pallas_call(
        functools.partial(accumulate, n, 80),
        out_shape=jax.ShapeDtypeStruct((cols, gout), F32),
        in_specs=[anywhere] * (2 * n + 1) + [pl.BlockSpec(memory_space=pltpu.VMEM)] * len(before),
        out_specs=pl.BlockSpec(memory_space=pltpu.VMEM),
        scratch_shapes=[
            pltpu.VMEM((n, rows, half), BF16),
            pltpu.VMEM((n, rows, half), BF16),
            pltpu.VMEM((kin, cols), BF16),
            pltpu.VMEM((cols, rows), BF16),
            pltpu.SemaphoreType.DMA((2 * n + 2,)),
        ],
        compiler_params=pltpu.CompilerParams(vmem_limit_bytes=60 << 20),
        cost_estimate=pl.CostEstimate(
            flops=2 * n * rows * kin * cols, bytes_accessed=4 * n * rows * half + 2 * kin * cols, transcendentals=0
        ),
    )(*lows, *highs, basis, *before)


def up(a, step):
    pairs = [(z * CORES + c, (z + step) % CHIPS * CORES + c) for z in range(CHIPS) for c in range(CORES)]
    return lax.ppermute(a, "own", pairs)


def swap(a):
    return lax.ppermute(a, "own", [(o, o ^ 1) for o in range(CHIPS * CORES)])


def balanced_basis(basis_slots, col_counts, img, own, groups, blk, wide):
    owners = CHIPS * CORES
    kin, cap = basis_slots.shape
    stripe = blk * owners
    ring = -(-cap // stripe) * stripe
    per = ring // owners
    depth = kin // groups
    starts = jnp.cumsum(col_counts) - col_counts
    z, c = own // CORES, own % CORES
    piece = lax.dynamic_slice(basis_slots, (img * depth, jnp.int32(0)), (depth, cap))
    slot = jnp.arange(cap, dtype=I32)
    place = (starts[own] + slot) % ring
    goal = place % stripe // blk
    hop = (goal // CORES - z) % CHIPS + CHIPS * ((goal % CORES) ^ c)
    place = jnp.where(slot < col_counts[own], hop * per + place // stripe * blk + place % blk, -1)
    send = jnp.arange(ring, dtype=I32)[:, None] == place[None, :]
    outgoing = lax.dot_general(send.astype(BF16), piece, (((1,), (1,)), ((), ())), preferred_element_type=F32)
    outgoing = outgoing.astype(BF16).reshape(CORES, CHIPS, per, depth)
    both = jnp.stack([outgoing[0], swap(outgoing[1])], axis=1)
    incoming = jnp.stack([both[0], up(both[1], 1), up(both[2], 2), up(both[3], -1)])
    source = ((z - jnp.arange(CHIPS, dtype=I32)) % CHIPS * CORES)[:, None] + (jnp.arange(CORES, dtype=I32) ^ c)[None, :]
    source = source.reshape(owners)
    begin, count = starts[source], col_counts[source]
    spot = jnp.arange(per, dtype=I32)
    at = spot // blk * stripe + own * blk + spot % blk
    offset = (at[None, :] - begin[:, None]) % ring
    column = begin[:, None] + offset
    target = jnp.where(offset < count[:, None], column // stripe * wide + column % blk, -1)
    keep = target.reshape(ring)[:, None] == jnp.arange(groups * wide, dtype=I32)[None, :]
    mine = lax.dot_general(
        incoming.reshape(ring, depth), keep.astype(BF16), (((0,), (0,)), ((), ())), preferred_element_type=F32
    )
    return lax.all_gather(mine.astype(BF16), "img", axis=0, tiled=True)


def gathered(low, high):
    low_down, high_up = up(low, 1), up(high, -1)
    low, high, low_down, high_up = lax.optimization_barrier((low, high, low_down, high_up))
    high_down, low_up = up(high, 1), up(low, -1)
    low_down, high_up, high_down, low_up = lax.optimization_barrier((low_down, high_up, high_down, low_up))
    low_far, high_far = up(low_down, 1), up(high_up, -1)
    lows, highs = [low, low_down, low_up, low_far], [high, high_down, high_up, high_far]
    lows = [b for a in lows for b in (a, swap(a))]
    highs = [b for a in highs for b in (a, swap(a))]
    return lows, highs


def shards(patches, grads, basis_g, basis_slots, col_counts):
    groups = lax.axis_size("img")
    owners = CHIPS * CORES
    img, own = lax.axis_index("img"), lax.axis_index("own")
    rows, kin = patches.shape
    gout = basis_g.shape[1]
    blk = kin // (groups * owners)
    proj = jnp.dot(grads, basis_g, preferred_element_type=F32).astype(BF16)
    half = (kin + gout) // 2
    low, high = patches[:, :half], jnp.concatenate([patches[:, half:], proj], axis=1)
    lows, highs = gathered(low, high)
    wide = -(-blk // 8) * 8
    basis = balanced_basis(basis_slots, col_counts, img, own, groups, blk, wide)
    near = len(lows) - CORES
    total = added(lows[:near], highs[:near], basis)
    total = added(lows[near:], highs[near:], basis, total)
    parts = lax.all_to_all(total.reshape(groups, wide, gout), "img", 0, 0, tiled=True)
    return jnp.sum(parts[:, :blk], axis=0) / F32(owners * rows // POS * groups)


def solution(mesh):
    in_specs = (P(("img", "own"), None), P(("img", "own"), None), P(), P(None, "own"), P())
    out_specs = P(("img", "own"), None)
    return jax.shard_map(shards, mesh=mesh, in_specs=in_specs, out_specs=out_specs, check_vma=False)
```

```python
import functools

import jax
import jax.numpy as jnp
from jax import lax
from jax.experimental import pallas as pl
from jax.experimental.pallas import tpu as pltpu
from jax.sharding import PartitionSpec as P

POS = 49
CHIPS = 4
CORES = 2
TOP = 13.0
F32, BF16, I32 = jnp.float32, jnp.bfloat16, jnp.int32


def accumulate(n, chunk, staged, block, *refs):
    lows, highs = refs[:n], refs[n : 2 * n]
    basis, *before, out, flip, total = refs[2 * n : len(refs) - (6 if staged else 0)]
    total = out if staged else total
    rows, half = lows[0].shape
    kin, cols = basis.shape
    rest = kin - half
    gout = half - rest
    parts = 4
    if staged:
        low, high, held, low_sems, high_sems, basis_sems = refs[-6:]
        lefts = [pltpu.make_async_copy(lows[k], low.at[k % 2], low_sems.at[k % 2]) for k in range(n)]
        rights = [pltpu.make_async_copy(highs[k], high.at[k % 2], high_sems.at[k % 2]) for k in range(n)]
        edges = [half * i // parts for i in range(parts)] + [half + rest * i // parts for i in range(parts + 1)]
        spans = [pl.ds(a, b - a) for a, b in zip(edges, edges[1:])]
        pieces = [pltpu.make_async_copy(basis.at[s], held.at[s], basis_sems.at[i]) for i, s in enumerate(spans)]
        lefts[0].start()
        for piece in pieces[:parts]:
            piece.start()
        rights[0].start()
        for piece in pieces[parts:]:
            piece.start()
        lows, highs, basis = [low.at[k % 2] for k in range(n)], [high.at[k % 2] for k in range(n)], held
    image = lax.broadcasted_iota(I32, (rows, gout), 0) // POS
    for k in range(n):
        if staged:
            lefts[k].wait()
            if k + 1 < n:
                lefts[k + 1].start()
        if staged and k == 0:
            proj = jnp.zeros((rows, cols), F32)
            for i in range(2 * parts):
                if i == parts:
                    rights[0].wait()
                    rights[1].start()
                pieces[i].wait()
                a, b = edges[i], edges[i + 1]
                left = lows[0][:, a:b] if i < parts else highs[0][:, a - half : b - half]
                proj += jnp.dot(left, basis[a:b], preferred_element_type=F32)
        else:
            proj = jnp.dot(lows[k][...], basis[:half], preferred_element_type=F32)
            if staged:
                rights[k].wait()
                if k + 1 < n:
                    rights[k + 1].start()
            proj += jnp.dot(highs[k][:, :rest], basis[half:], preferred_element_type=F32)
        flip[k % 2] = proj.astype(BF16).T
        grads = highs[k][:, rest:]
        apart = [jnp.where(image == m, grads, jnp.zeros_like(grads)) for m in range(rows // POS)]
        source = total if k else before[0] if before else None
        for s in range(0, cols, chunk):
            left = flip[k % 2, s : s + chunk]
            squares = jnp.zeros((chunk, gout), F32) if source is None else source[s : s + chunk]
            for one in apart:
                coef = jnp.dot(left, one, preferred_element_type=F32)
                squares += coef * coef
            total[s : s + chunk] = squares
    if not staged:
        peak = jnp.max(jnp.max(total[...], axis=0, keepdims=True), axis=1, keepdims=True)
        level = jnp.floor(jnp.log(jnp.maximum(peak, 1e-30)) * 1.4426950408889634)
        row = lax.rem(lax.broadcasted_iota(I32, (cols, gout), 0), jnp.int32(block[1]))
        out[...] = jnp.where(row == block[0], level, total[...] * jnp.exp2(TOP - level))


def added(lows, highs, basis, *before, staged=False, block=()):
    n = len(lows)
    rows, half = lows[0].shape
    kin, cols = basis.shape
    gout = 2 * half - kin
    inside = pl.BlockSpec(memory_space=pltpu.VMEM)
    source = pl.BlockSpec(memory_space=pltpu.HBM) if staged else inside
    room = [
        pltpu.VMEM((2, rows, half), BF16),
        pltpu.VMEM((2, rows, half), BF16),
        pltpu.VMEM((kin, cols), BF16),
        pltpu.SemaphoreType.DMA((2,)),
        pltpu.SemaphoreType.DMA((2,)),
        pltpu.SemaphoreType.DMA((8,)),
    ]
    return pl.pallas_call(
        functools.partial(accumulate, n, cols // 2, staged, block),
        out_shape=jax.ShapeDtypeStruct((cols, gout), F32),
        in_specs=[source] * (2 * n + 1) + [inside] * len(before),
        out_specs=inside,
        scratch_shapes=[pltpu.VMEM((2, cols, rows), BF16), pltpu.VMEM((8, 128) if staged else (cols, gout), F32)]
        + (room if staged else []),
        compiler_params=pltpu.CompilerParams(vmem_limit_bytes=(60 if staged else 28) << 20),
        cost_estimate=pl.CostEstimate(
            flops=2 * n * rows * kin * cols, bytes_accessed=4 * n * rows * half + 2 * kin * cols, transcendentals=0
        ),
    )(*lows, *highs, basis, *before)


def place(blk, ring, me, counts, slots, kept, given, held, sem):
    depth, cap = held.shape
    owners = CHIPS * CORES
    stripe, per = blk * owners, ring // owners
    img, own = me[0], me[1]
    z, c = own // CORES, own % CORES
    copy = pltpu.make_async_copy(slots.at[pl.ds(pl.multiple_of(img * depth, 16), depth)], held, sem)
    copy.start()
    start = jnp.int32(0)
    for o in range(owners):
        start += jnp.where(o < own, counts[o], 0)
    slot = lax.broadcasted_iota(I32, (1, cap), 1)
    spot = lax.rem(start + slot, jnp.int32(ring))
    goal = lax.div(lax.rem(spot, jnp.int32(stripe)), jnp.int32(blk))
    hop = ((goal // CORES - z + CHIPS) & (CHIPS - 1)) + CHIPS * ((goal & 1) ^ c)
    row = hop * per + lax.div(spot, jnp.int32(stripe)) * blk + lax.rem(spot, jnp.int32(blk))
    row = jnp.where(slot < counts[own], row, -1)
    copy.wait()
    for r in range(0, ring, per):
        here = lax.broadcasted_iota(I32, (per, cap), 0) + r == row
        out = kept if r < ring // CORES else given
        out[r % (ring // CORES) // per] = lax.dot_general(
            here.astype(F32).astype(BF16), held[...], (((1,), (1,)), ((), ())), preferred_element_type=F32
        ).astype(BF16)


def placed(basis_slots, col_counts, img, own, groups, blk, ring):
    kin, cap = basis_slots.shape
    depth = kin // groups
    scalars = pl.BlockSpec(memory_space=pltpu.SMEM)
    return pl.pallas_call(
        functools.partial(place, blk, ring),
        out_shape=[jax.ShapeDtypeStruct((CHIPS, ring // CHIPS // CORES, depth), BF16)] * CORES,
        in_specs=[scalars, scalars, pl.BlockSpec(memory_space=pltpu.HBM)],
        out_specs=[pl.BlockSpec(memory_space=pltpu.VMEM)] * CORES,
        scratch_shapes=[pltpu.VMEM((depth, cap), BF16), pltpu.SemaphoreType.DMA],
        compiler_params=pltpu.CompilerParams(vmem_limit_bytes=55 << 20),
        cost_estimate=pl.CostEstimate(flops=2 * ring * cap * depth, bytes_accessed=4 * depth * cap, transcendentals=0),
    )(jnp.stack([img, own]).astype(I32), col_counts, basis_slots)


def up(a, step):
    pairs = [(z * CORES + c, (z + step) % CHIPS * CORES + c) for z in range(CHIPS) for c in range(CORES)]
    return lax.ppermute(a, "own", pairs)


def swap(a):
    return lax.ppermute(a, "own", [(o, o ^ 1) for o in range(CHIPS * CORES)])


def balanced_basis(basis_slots, col_counts, img, own, groups, blk, wide):
    owners = CHIPS * CORES
    kin, cap = basis_slots.shape
    stripe = blk * owners
    ring = -(-cap // stripe) * stripe
    per = ring // owners
    depth = kin // groups
    starts = jnp.cumsum(col_counts) - col_counts
    z, c = own // CORES, own % CORES
    kept, given = placed(basis_slots, col_counts, img, own, groups, blk, ring)
    both = jnp.stack([kept, swap(given)], axis=1)
    incoming = jnp.stack([both[0], up(both[1], 1), up(both[2], 2), up(both[3], -1)])
    source = ((z - jnp.arange(CHIPS, dtype=I32)) % CHIPS * CORES)[:, None] + (jnp.arange(CORES, dtype=I32) ^ c)[None, :]
    source = source.reshape(owners)
    begin, count = starts[source], col_counts[source]
    spot = jnp.arange(per, dtype=I32)
    at = spot // blk * stripe + own * blk + spot % blk
    offset = (at[None, :] - begin[:, None]) % ring
    column = begin[:, None] + offset
    target = jnp.where(offset < count[:, None], column // stripe * wide + column % blk, -1)
    keep = target.reshape(ring)[:, None] == jnp.arange(groups * wide, dtype=I32)[None, :]
    mine = lax.dot_general(
        incoming.reshape(ring, depth), keep.astype(BF16), (((0,), (0,)), ((), ())), preferred_element_type=F32
    )
    return lax.all_gather(mine.astype(BF16), "img", axis=0, tiled=True)


def gathered(low, high):
    low_down, high_up = up(low, 1), up(high, -1)
    low, high, low_down, high_up = lax.optimization_barrier((low, high, low_down, high_up))
    high_down, low_up = up(high, 1), up(low, -1)
    low_down, high_up, high_down, low_up = lax.optimization_barrier((low_down, high_up, high_down, low_up))
    low_far, high_far = up(low_down, 1), up(high_up, -1)
    return [low, low_down, low_up, low_far], [high, high_down, high_up, high_far]


def shared(arrays):
    return [b for a in arrays for b in (a, swap(a))]


def shards(patches, grads, basis_g, basis_slots, col_counts):
    groups = lax.axis_size("img")
    owners = CHIPS * CORES
    img, own = lax.axis_index("img"), lax.axis_index("own")
    rows, kin = patches.shape
    gout = basis_g.shape[1]
    blk = kin // (groups * owners)
    proj = jnp.dot(grads, basis_g, preferred_element_type=F32).astype(BF16)
    half = (kin + gout) // 2
    low, high = patches[:, :half], jnp.concatenate([patches[:, half:], proj], axis=1)
    lows, highs = gathered(low, high)
    wide = -(-(blk + 1) // 8) * 8
    basis = balanced_basis(basis_slots, col_counts, img, own, groups, blk, wide)
    total = added(shared(lows[:-1]), shared(highs[:-1]), basis, staged=True)
    low, high, total = lax.optimization_barrier((lows[-1], highs[-1], total))
    total = added(shared([low]), shared([high]), basis, total, block=(blk, wide))
    parts = lax.all_to_all(total.astype(jnp.float16).reshape(groups, wide, gout), "img", 0, 0, tiled=True)
    level = parts[:, blk : blk + 1, :1].astype(F32) - TOP
    return jnp.sum(parts[:, :blk].astype(F32) * jnp.exp2(level), axis=0) / F32(owners * rows // POS * groups)


def solution(mesh):
    in_specs = (P(("img", "own"), None), P(("img", "own"), None), P(), P(None, "own"), P())
    out_specs = P(("img", "own"), None)
    return jax.shard_map(shards, mesh=mesh, in_specs=in_specs, out_specs=out_specs, check_vma=False)
```

```python
import functools

import jax
import jax.numpy as jnp
from jax import lax
from jax.experimental import pallas as pl
from jax.experimental.pallas import tpu as pltpu
from jax.sharding import PartitionSpec as P

POS = 49
CHIPS = 4
CORES = 2
TOP = 13.0
LIMITS = {"near": 54, "far": 28, "last": 28}
F32, BF16, I32 = jnp.float32, jnp.bfloat16, jnp.int32


def accumulate(n, chunk, mode, block, *refs):
    lows, highs = refs[:n], refs[n : 2 * n]
    staged = mode == "near"
    before = []
    if staged:
        basis, total, flip, held, basis_sems, low, high, low_sems, high_sems = refs[2 * n :]
    elif mode == "far":
        basis, total, flip = refs[2 * n :]
    else:
        basis, *before, out, flip, total = refs[2 * n :]
    rows, half = lows[0].shape
    kin, cols = basis.shape
    rest = kin - half
    gout = half - rest
    parts = 2
    if staged:
        lefts = [pltpu.make_async_copy(lows[k], low.at[k % 2], low_sems.at[k % 2]) for k in range(n)]
        rights = [pltpu.make_async_copy(highs[k], high.at[k % 2], high_sems.at[k % 2]) for k in range(n)]
        lows, highs = [low.at[k % 2] for k in range(n)], [high.at[k % 2] for k in range(n)]
        lefts[0].start()
        edges = [half * i // parts for i in range(parts)] + [half + rest * i // parts for i in range(parts + 1)]
        spans = [pl.ds(a, b - a) for a, b in zip(edges, edges[1:])]
        pieces = [pltpu.make_async_copy(basis.at[s], held.at[s], basis_sems.at[i]) for i, s in enumerate(spans)]
        for i, piece in enumerate(pieces):
            if i == parts:
                rights[0].start()
            piece.start()
        basis = held
    image = lax.broadcasted_iota(I32, (rows, gout), 0) // POS
    for k in range(n):
        if staged:
            lefts[k].wait()
            if k + 1 < n:
                lefts[k + 1].start()
        if staged and k == 0:
            proj = jnp.zeros((rows, cols), F32)
            for i in range(2 * parts):
                if i == parts:
                    rights[0].wait()
                    rights[1].start()
                pieces[i].wait()
                a, b = edges[i], edges[i + 1]
                left = lows[0][:, a:b] if i < parts else highs[0][:, a - half : b - half]
                proj += jnp.dot(left, basis[a:b], preferred_element_type=F32)
        else:
            proj = jnp.dot(lows[k][...], basis[:half], preferred_element_type=F32)
            if staged:
                rights[k].wait()
                if k + 1 < n:
                    rights[k + 1].start()
            proj += jnp.dot(highs[k][:, :rest], basis[half:], preferred_element_type=F32)
        flip[k % 2] = proj.astype(BF16).T
        grads = highs[k][:, rest:]
        apart = [jnp.where(image == m, grads, jnp.zeros_like(grads)) for m in range(rows // POS)]
        sources = [total] if k else before
        for s in range(0, cols, chunk):
            left = flip[k % 2, s : s + chunk]
            squares = jnp.zeros((chunk, gout), F32)
            for source in sources:
                squares += source[s : s + chunk]
            for one in apart:
                coef = jnp.dot(left, one, preferred_element_type=F32)
                squares += coef * coef
            total[s : s + chunk] = squares
    if block:
        peak = jnp.max(jnp.max(total[...], axis=0, keepdims=True), axis=1, keepdims=True)
        level = jnp.floor(jnp.log(jnp.maximum(peak, 1e-30)) * 1.4426950408889634)
        row = lax.rem(lax.broadcasted_iota(I32, (cols, gout), 0), jnp.int32(block[1]))
        out[...] = jnp.where(row == block[0], level, total[...] * jnp.exp2(TOP - level))


def added(mode, pairs, basis, *before, block=()):
    n = len(pairs)
    lows, highs = zip(*pairs)
    rows, half = lows[0].shape
    kin, cols = basis.shape
    gout = 2 * half - kin
    inside, outside = pl.BlockSpec(memory_space=pltpu.VMEM), pl.BlockSpec(memory_space=pltpu.HBM)
    room = [pltpu.VMEM((2, cols, rows), BF16)]
    if mode == "near":
        pair, sems = pltpu.VMEM((2, rows, half), BF16), pltpu.SemaphoreType.DMA
        room += [pltpu.VMEM((kin, cols), BF16), sems((4,)), pair, pair, sems((2,)), sems((2,))]
    elif mode == "last":
        room += [pltpu.VMEM((cols, gout), F32)]
    return pl.pallas_call(
        functools.partial(accumulate, n, cols // 2, mode, block),
        out_shape=jax.ShapeDtypeStruct((cols, gout), F32),
        in_specs=[outside if mode == "near" else inside] * (2 * n + 1) + [inside] * len(before),
        out_specs=inside,
        scratch_shapes=room,
        compiler_params=pltpu.CompilerParams(vmem_limit_bytes=LIMITS[mode] << 20),
        cost_estimate=pl.CostEstimate(
            flops=2 * n * rows * kin * cols, bytes_accessed=4 * n * rows * half + 2 * kin * cols, transcendentals=0
        ),
    )(*lows, *highs, basis, *before)


def place(blk, ring, me, counts, slots, kept, given, held, hot, sem):
    depth, cap = held.shape
    owners = CHIPS * CORES
    stripe, per = blk * owners, ring // owners
    img, own = me[0], me[1]
    z, c = own // CORES, own % CORES
    copy = pltpu.make_async_copy(slots.at[pl.ds(pl.multiple_of(img * depth, 16), depth)], held, sem)
    copy.start()
    start = jnp.int32(0)
    for o in range(owners):
        start += jnp.where(o < own, counts[o], 0)
    slot = lax.broadcasted_iota(I32, (1, cap), 1)
    spot = lax.rem(start + slot, jnp.int32(ring))
    goal = lax.div(lax.rem(spot, jnp.int32(stripe)), jnp.int32(blk))
    hop = ((goal // CORES - z + CHIPS) & (CHIPS - 1)) + CHIPS * ((goal & 1) ^ c)
    row = hop * per + lax.div(spot, jnp.int32(stripe)) * blk + lax.rem(spot, jnp.int32(blk))
    row = jnp.where(slot < counts[own], row, -1)
    for r in range(0, ring, per):
        here = lax.broadcasted_iota(I32, (per, cap), 0) + r == row
        hot[r : r + per] = here.astype(F32).astype(BF16)
    copy.wait()
    laid = lax.dot_general(hot[...], held[...], (((1,), (1,)), ((), ())), preferred_element_type=F32).astype(BF16)
    for r in range(0, ring, per):
        out = kept if r < ring // CORES else given
        out[r % (ring // CORES) // per] = laid[r : r + per]


def placed(basis_slots, col_counts, img, own, groups, blk, ring):
    kin, cap = basis_slots.shape
    depth = kin // groups
    scalars = pl.BlockSpec(memory_space=pltpu.SMEM)
    return pl.pallas_call(
        functools.partial(place, blk, ring),
        out_shape=[jax.ShapeDtypeStruct((CHIPS, ring // CHIPS // CORES, depth), BF16)] * CORES,
        in_specs=[scalars, scalars, pl.BlockSpec(memory_space=pltpu.HBM)],
        out_specs=[pl.BlockSpec(memory_space=pltpu.VMEM)] * CORES,
        scratch_shapes=[pltpu.VMEM((depth, cap), BF16), pltpu.VMEM((ring, cap), BF16), pltpu.SemaphoreType.DMA],
        compiler_params=pltpu.CompilerParams(vmem_limit_bytes=55 << 20),
        cost_estimate=pl.CostEstimate(flops=2 * ring * cap * depth, bytes_accessed=4 * depth * cap, transcendentals=0),
    )(jnp.stack([img, own]).astype(I32), col_counts, basis_slots)


def up(a, step):
    pairs = [(z * CORES + c, (z + step) % CHIPS * CORES + c) for z in range(CHIPS) for c in range(CORES)]
    return lax.ppermute(a, "own", pairs)


def swap(a):
    return lax.ppermute(a, "own", [(o, o ^ 1) for o in range(CHIPS * CORES)])


def balanced_basis(basis_slots, col_counts, img, own, groups, blk, wide):
    owners = CHIPS * CORES
    kin, cap = basis_slots.shape
    stripe = blk * owners
    ring = -(-cap // stripe) * stripe
    per = ring // owners
    depth = kin // groups
    starts = jnp.cumsum(col_counts) - col_counts
    z, c = own // CORES, own % CORES
    kept, given = placed(basis_slots, col_counts, img, own, groups, blk, ring)
    both = jnp.stack([kept, swap(given)], axis=1)
    incoming = jnp.stack([both[0], up(both[1], 1), up(both[2], 2), up(both[3], -1)])
    source = ((z - jnp.arange(CHIPS, dtype=I32)) % CHIPS * CORES)[:, None] + (jnp.arange(CORES, dtype=I32) ^ c)[None, :]
    source = source.reshape(owners)
    begin, count = starts[source], col_counts[source]
    spot = jnp.arange(per, dtype=I32)
    at = spot // blk * stripe + own * blk + spot % blk
    offset = (at[None, :] - begin[:, None]) % ring
    column = begin[:, None] + offset
    target = jnp.where(offset < count[:, None], column // stripe * wide + column % blk, -1)
    keep = target.reshape(ring)[:, None] == jnp.arange(groups * wide, dtype=I32)[None, :]
    mine = lax.dot_general(
        incoming.reshape(ring, depth), keep.astype(BF16), (((0,), (0,)), ((), ())), preferred_element_type=F32
    )
    return lax.all_gather(mine.astype(BF16), "img", axis=0, tiled=True)


def gathered(low, high):
    low_down, high_up = up(low, 1), up(high, -1)
    mine = (low, high, swap(low), swap(high))
    low, high, low_down, high_up, mine = lax.optimization_barrier((low, high, low_down, high_up, mine))
    high_down, low_up = up(high, 1), up(low, -1)
    other_low, other_high = swap(low_down), swap(high_up)
    low_down, high_up, high_down, low_up, other_low, other_high = lax.optimization_barrier(
        (low_down, high_up, high_down, low_up, other_low, other_high)
    )
    far = (up(low_down, 1), up(high_up, -1))
    pairs = [mine[:2], mine[2:], (low_down, high_down), (other_low, swap(high_down)), (low_up, high_up)]
    return pairs + [(swap(low_up), other_high)], far


def shards(patches, grads, basis_g, basis_slots, col_counts):
    groups = lax.axis_size("img")
    owners = CHIPS * CORES
    img, own = lax.axis_index("img"), lax.axis_index("own")
    rows, kin = patches.shape
    gout = basis_g.shape[1]
    blk = kin // (groups * owners)
    proj = jnp.dot(grads, basis_g, preferred_element_type=F32).astype(BF16)
    half = (kin + gout) // 2
    low, high = patches[:, :half], jnp.concatenate([patches[:, half:], proj], axis=1)
    near, far = gathered(low, high)
    wide = -(-(blk + 1) // 8) * 8
    basis = balanced_basis(basis_slots, col_counts, img, own, groups, blk, wide)
    sums = added("near", near, basis)
    far, sums = lax.optimization_barrier((far, sums))
    partner = swap(far[0]), swap(far[1])
    more = added("far", [far], basis)
    total = added("last", [partner], basis, more, sums, block=(blk, wide))
    parts = lax.all_to_all(total.astype(jnp.float16).reshape(groups, wide, gout), "img", 0, 0, tiled=True)
    level = parts[:, blk : blk + 1, :1].astype(F32) - TOP
    return jnp.sum(parts[:, :blk].astype(F32) * jnp.exp2(level), axis=0) / F32(owners * rows // POS * groups)


def solution(mesh):
    in_specs = (P(("img", "own"), None), P(("img", "own"), None), P(), P(None, "own"), P())
    out_specs = P(("img", "own"), None)
    return jax.shard_map(shards, mesh=mesh, in_specs=in_specs, out_specs=out_specs, check_vma=False)
```

```python
import functools

import jax
import jax.numpy as jnp
from jax import lax
from jax.experimental import pallas as pl
from jax.experimental.pallas import tpu as pltpu
from jax.sharding import PartitionSpec as P

POS = 49
CHIPS = 4
CORES = 2
TOP = 13.0
LIMITS = {"near": 54, "far": 28, "last": 28}
F32, BF16, I32 = jnp.float32, jnp.bfloat16, jnp.int32


def accumulate(n, chunk, mode, block, *refs):
    lows, highs = refs[:n], refs[n : 2 * n]
    staged = mode == "near"
    before = []
    if staged:
        basis, total, flip, held, basis_sems, low, high, low_sems, high_sems = refs[2 * n :]
    elif mode == "far":
        basis, total, flip = refs[2 * n :]
    else:
        basis, *before, out, flip, total = refs[2 * n :]
    rows, half = lows[0].shape
    kin, cols = basis.shape
    rest = kin - half
    gout = half - rest
    parts = 2
    if staged:
        lefts = [pltpu.make_async_copy(lows[k], low.at[k % 2], low_sems.at[k % 2]) for k in range(n)]
        rights = [pltpu.make_async_copy(highs[k], high.at[k % 2], high_sems.at[k % 2]) for k in range(n)]
        lows, highs = [low.at[k % 2] for k in range(n)], [high.at[k % 2] for k in range(n)]
        lefts[0].start()
        edges = [half * i // parts for i in range(parts)] + [half + rest * i // parts for i in range(parts + 1)]
        spans = [pl.ds(a, b - a) for a, b in zip(edges, edges[1:])]
        pieces = [pltpu.make_async_copy(basis.at[s], held.at[s], basis_sems.at[i]) for i, s in enumerate(spans)]
        for i, piece in enumerate(pieces):
            if i == parts:
                rights[0].start()
            piece.start()
        basis = held
    image = lax.broadcasted_iota(I32, (rows, gout), 0) // POS
    for k in range(n):
        if staged:
            lefts[k].wait()
            if k + 1 < n:
                lefts[k + 1].start()
        if staged and k == 0:
            proj = jnp.zeros((rows, cols), F32)
            for i in range(2 * parts):
                if i == parts:
                    rights[0].wait()
                    rights[1].start()
                pieces[i].wait()
                a, b = edges[i], edges[i + 1]
                left = lows[0][:, a:b] if i < parts else highs[0][:, a - half : b - half]
                proj += jnp.dot(left, basis[a:b], preferred_element_type=F32)
        else:
            proj = jnp.dot(lows[k][...], basis[:half], preferred_element_type=F32)
            if staged:
                rights[k].wait()
                if k + 1 < n:
                    rights[k + 1].start()
            proj += jnp.dot(highs[k][:, :rest], basis[half:], preferred_element_type=F32)
        flip[k % 2] = proj.astype(BF16).T
        grads = highs[k][:, rest:]
        apart = [jnp.where(image == m, grads, jnp.zeros_like(grads)) for m in range(rows // POS)]
        sources = [total] if k else before
        for s in range(0, cols, chunk):
            left = flip[k % 2, s : s + chunk]
            squares = jnp.zeros((chunk, gout), F32)
            for source in sources:
                squares += source[s : s + chunk]
            for one in apart:
                coef = jnp.dot(left, one, preferred_element_type=F32)
                squares += coef * coef
            total[s : s + chunk] = squares
    if block:
        peak = jnp.max(jnp.max(total[...], axis=0, keepdims=True), axis=1, keepdims=True)
        level = jnp.floor(jnp.log(jnp.maximum(peak, 1e-30)) * 1.4426950408889634)
        row = lax.rem(lax.broadcasted_iota(I32, (cols, gout), 0), jnp.int32(block[1]))
        out[...] = jnp.where(row == block[0], level, total[...] * jnp.exp2(TOP - level))


def added(mode, pairs, basis, *before, block=()):
    n = len(pairs)
    lows, highs = zip(*pairs)
    rows, half = lows[0].shape
    kin, cols = basis.shape
    gout = 2 * half - kin
    inside, outside = pl.BlockSpec(memory_space=pltpu.VMEM), pl.BlockSpec(memory_space=pltpu.HBM)
    room = [pltpu.VMEM((2, cols, rows), BF16)]
    if mode == "near":
        pair, sems = pltpu.VMEM((2, rows, half), BF16), pltpu.SemaphoreType.DMA
        room += [pltpu.VMEM((kin, cols), BF16), sems((4,)), pair, pair, sems((2,)), sems((2,))]
    elif mode == "last":
        room += [pltpu.VMEM((cols, gout), F32)]
    return pl.pallas_call(
        functools.partial(accumulate, n, cols // 2, mode, block),
        out_shape=jax.ShapeDtypeStruct((cols, gout), F32),
        in_specs=[outside if mode == "near" else inside] * (2 * n + 1) + [inside] * len(before),
        out_specs=inside,
        scratch_shapes=room,
        compiler_params=pltpu.CompilerParams(vmem_limit_bytes=LIMITS[mode] << 20),
        cost_estimate=pl.CostEstimate(
            flops=2 * n * rows * kin * cols, bytes_accessed=4 * n * rows * half + 2 * kin * cols, transcendentals=0
        ),
    )(*lows, *highs, basis, *before)


def place(blk, ring, me, counts, slots, *refs):
    *hops, hot = refs
    cap = slots.shape[1]
    owners = CHIPS * CORES
    stripe, per = blk * owners, ring // owners
    own = me[0]
    z, c = own // CORES, own % CORES
    start = jnp.int32(0)
    for o in range(owners):
        start += jnp.where(o < own, counts[o], 0)
    slot = lax.broadcasted_iota(I32, (1, cap), 1)
    spot = lax.rem(start + slot, jnp.int32(ring))
    goal = lax.div(lax.rem(spot, jnp.int32(stripe)), jnp.int32(blk))
    hop = ((goal // CORES - z + CHIPS) & (CHIPS - 1)) * CORES + ((goal & 1) ^ c)
    row = hop * per + lax.div(spot, jnp.int32(stripe)) * blk + lax.rem(spot, jnp.int32(blk))
    row = jnp.where(slot < counts[own], row, -1)
    for r in range(0, ring, per):
        here = lax.broadcasted_iota(I32, (per, cap), 0) + r == row
        hot[r : r + per] = here.astype(F32).astype(BF16)
    laid = lax.dot_general(hot[...], slots[...], (((1,), (1,)), ((), ())), preferred_element_type=F32).astype(BF16)
    for r in range(0, ring, per):
        hops[r // per // CORES][r // per % CORES] = laid[r : r + per]


def placed(basis_slots, col_counts, img, own, groups, blk, ring):
    kin, cap = basis_slots.shape
    depth = kin // groups
    piece = lax.dynamic_slice(basis_slots, (img * depth, jnp.int32(0)), (depth, cap))
    scalars, inside = pl.BlockSpec(memory_space=pltpu.SMEM), pl.BlockSpec(memory_space=pltpu.VMEM)
    return pl.pallas_call(
        functools.partial(place, blk, ring),
        out_shape=[jax.ShapeDtypeStruct((CORES, ring // CHIPS // CORES, depth), BF16)] * CHIPS,
        in_specs=[scalars, scalars, inside],
        out_specs=[inside] * CHIPS,
        scratch_shapes=[pltpu.VMEM((ring, cap), BF16)],
        compiler_params=pltpu.CompilerParams(vmem_limit_bytes=28 << 20),
        cost_estimate=pl.CostEstimate(flops=2 * ring * cap * depth, bytes_accessed=4 * depth * cap, transcendentals=0),
    )(own.astype(I32).reshape(1), col_counts, piece)


def up(a, step):
    pairs = [(z * CORES + c, (z + step) % CHIPS * CORES + c) for z in range(CHIPS) for c in range(CORES)]
    return lax.ppermute(a, "own", pairs)


def swap(a):
    return lax.ppermute(a, "own", [(o, o ^ 1) for o in range(CHIPS * CORES)])


def balanced_basis(basis_slots, col_counts, img, own, groups, blk, wide, first):
    owners = CHIPS * CORES
    kin, cap = basis_slots.shape
    stripe = blk * owners
    ring = -(-cap // stripe) * stripe
    per = ring // owners
    depth = kin // groups
    starts = jnp.cumsum(col_counts) - col_counts
    z, c = own // CORES, own % CORES
    hops = placed(basis_slots, col_counts, img, own, groups, blk, ring)
    hops = [hops[0], up(hops[1], 1), up(hops[2], 2), up(hops[3], -1)]
    hops, first = lax.optimization_barrier((hops, first))
    given = swap(jnp.stack([hop[1] for hop in hops]))
    incoming = jnp.concatenate([jnp.stack([hop[0] for hop in hops]), given])
    source = (z - jnp.arange(CHIPS, dtype=I32)) % CHIPS * CORES
    source = jnp.concatenate([source + c, source + (c ^ 1)])
    begin, count = starts[source], col_counts[source]
    spot = jnp.arange(per, dtype=I32)
    at = spot // blk * stripe + own * blk + spot % blk
    offset = (at[None, :] - begin[:, None]) % ring
    column = begin[:, None] + offset
    target = jnp.where(offset < count[:, None], column // stripe * wide + column % blk, -1)
    keep = target.reshape(ring)[:, None] == jnp.arange(groups * wide, dtype=I32)[None, :]
    mine = lax.dot_general(
        incoming.reshape(ring, depth), keep.astype(BF16), (((0,), (0,)), ((), ())), preferred_element_type=F32
    )
    return lax.all_gather(mine.astype(BF16), "img", axis=0, tiled=True), first


def gathered(low, high):
    low_down, high_up = up(low, 1), up(high, -1)
    mine = (low, high, swap(low), swap(high))
    low, high, low_down, high_up, mine = lax.optimization_barrier((low, high, low_down, high_up, mine))
    high_down, low_up = up(high, 1), up(low, -1)
    other_low, other_high = swap(low_down), swap(high_up)
    low_down, high_up, high_down, low_up, other_low, other_high = lax.optimization_barrier(
        (low_down, high_up, high_down, low_up, other_low, other_high)
    )
    far = (up(low_down, 1), up(high_up, -1))
    pairs = [mine[:2], mine[2:], (low_down, high_down), (other_low, swap(high_down)), (low_up, high_up)]
    return pairs + [(swap(low_up), other_high)], far


def shards(patches, grads, basis_g, basis_slots, col_counts):
    groups = lax.axis_size("img")
    owners = CHIPS * CORES
    img, own = lax.axis_index("img"), lax.axis_index("own")
    rows, kin = patches.shape
    gout = basis_g.shape[1]
    blk = kin // (groups * owners)
    proj = jnp.dot(grads, basis_g, preferred_element_type=F32).astype(BF16)
    half = (kin + gout) // 2
    low, high = patches[:, :half], jnp.concatenate([patches[:, half:], proj], axis=1)
    wide = -(-(blk + 1) // 8) * 8
    basis, (low, high) = balanced_basis(basis_slots, col_counts, img, own, groups, blk, wide, (low, high))
    near, far = gathered(low, high)
    sums = added("near", near, basis)
    far, sums = lax.optimization_barrier((far, sums))
    partner = swap(far[0]), swap(far[1])
    more = added("far", [far], basis)
    total = added("last", [partner], basis, more, sums, block=(blk, wide))
    parts = lax.all_to_all(total.astype(jnp.float16).reshape(groups, wide, gout), "img", 0, 0, tiled=True)
    level = parts[:, blk : blk + 1, :1].astype(F32) - TOP
    return jnp.sum(parts[:, :blk].astype(F32) * jnp.exp2(level), axis=0) / F32(owners * rows // POS * groups)


def solution(mesh):
    in_specs = (P(("img", "own"), None), P(("img", "own"), None), P(), P(None, "own"), P())
    out_specs = P(("img", "own"), None)
    return jax.shard_map(shards, mesh=mesh, in_specs=in_specs, out_specs=out_specs, check_vma=False)
```

```python
import functools

import jax
import jax.numpy as jnp
from jax import lax
from jax.experimental import pallas as pl
from jax.experimental.pallas import tpu as pltpu
from jax.sharding import PartitionSpec as P

POS = 49
CHIPS = 4
CORES = 2
TOP = 13.0
LIMITS = {"near": 54, "far": 28, "last": 28}
F32, BF16, I32 = jnp.float32, jnp.bfloat16, jnp.int32


def accumulate(n, chunk, mode, block, *refs):
    lows, highs = refs[:n], refs[n : 2 * n]
    staged = mode == "near"
    before = []
    if staged:
        basis, total, flip, held, basis_sems, low, high, low_sems, high_sems = refs[2 * n :]
    elif mode == "far":
        basis, total, flip = refs[2 * n :]
    else:
        basis, *before, out, flip, total = refs[2 * n :]
    rows, half = lows[0].shape
    kin, cols = basis.shape
    rest = kin - half
    gout = half - rest
    parts = 2
    if staged:
        lefts = [pltpu.make_async_copy(lows[k], low.at[k % 2], low_sems.at[k % 2]) for k in range(n)]
        rights = [pltpu.make_async_copy(highs[k], high.at[k % 2], high_sems.at[k % 2]) for k in range(n)]
        lows, highs = [low.at[k % 2] for k in range(n)], [high.at[k % 2] for k in range(n)]
        lefts[0].start()
        edges = [half * i // parts for i in range(parts)] + [half + rest * i // parts for i in range(parts + 1)]
        spans = [pl.ds(a, b - a) for a, b in zip(edges, edges[1:])]
        pieces = [pltpu.make_async_copy(basis.at[s], held.at[s], basis_sems.at[i]) for i, s in enumerate(spans)]
        for i, piece in enumerate(pieces):
            if i == parts:
                rights[0].start()
            piece.start()
        basis = held
    image = lax.broadcasted_iota(I32, (rows, gout), 0) // POS
    for k in range(n):
        if staged:
            lefts[k].wait()
            if k + 1 < n:
                lefts[k + 1].start()
        if staged and k == 0:
            proj = jnp.zeros((rows, cols), F32)
            for i in range(2 * parts):
                if i == parts:
                    rights[0].wait()
                    rights[1].start()
                pieces[i].wait()
                a, b = edges[i], edges[i + 1]
                left = lows[0][:, a:b] if i < parts else highs[0][:, a - half : b - half]
                proj += jnp.dot(left, basis[a:b], preferred_element_type=F32)
        else:
            proj = jnp.dot(lows[k][...], basis[:half], preferred_element_type=F32)
            if staged:
                rights[k].wait()
                if k + 1 < n:
                    rights[k + 1].start()
            proj += jnp.dot(highs[k][:, :rest], basis[half:], preferred_element_type=F32)
        flip[k % 2] = proj.astype(BF16).T
        grads = highs[k][:, rest:]
        apart = [jnp.where(image == m, grads, jnp.zeros_like(grads)) for m in range(rows // POS)]
        sources = [total] if k else before
        for s in range(0, cols, chunk):
            left = flip[k % 2, s : s + chunk]
            squares = jnp.zeros((chunk, gout), F32)
            for source in sources:
                squares += source[s : s + chunk]
            for one in apart:
                coef = jnp.dot(left, one, preferred_element_type=F32)
                squares += coef * coef
            total[s : s + chunk] = squares
    if block:
        peak = jnp.max(jnp.max(total[...], axis=0, keepdims=True), axis=1, keepdims=True)
        level = jnp.floor(jnp.log(jnp.maximum(peak, 1e-30)) * 1.4426950408889634)
        row = lax.rem(lax.broadcasted_iota(I32, (cols, gout), 0), jnp.int32(block[1]))
        out[...] = jnp.where(row == block[0], level, total[...] * jnp.exp2(TOP - level))


def added(mode, pairs, basis, *before, block=()):
    n = len(pairs)
    lows, highs = zip(*pairs)
    rows, half = lows[0].shape
    kin, cols = basis.shape
    gout = 2 * half - kin
    inside, outside = pl.BlockSpec(memory_space=pltpu.VMEM), pl.BlockSpec(memory_space=pltpu.HBM)
    room = [pltpu.VMEM((2, cols, rows), BF16)]
    if mode == "near":
        pair, sems = pltpu.VMEM((2, rows, half), BF16), pltpu.SemaphoreType.DMA
        room += [pltpu.VMEM((kin, cols), BF16), sems((4,)), pair, pair, sems((2,)), sems((2,))]
    elif mode == "last":
        room += [pltpu.VMEM((cols, gout), F32)]
    return pl.pallas_call(
        functools.partial(accumulate, n, cols // 2, mode, block),
        out_shape=jax.ShapeDtypeStruct((cols, gout), F32),
        in_specs=[outside if mode == "near" else inside] * (2 * n + 1) + [inside] * len(before),
        out_specs=inside,
        scratch_shapes=room,
        compiler_params=pltpu.CompilerParams(vmem_limit_bytes=LIMITS[mode] << 20),
        cost_estimate=pl.CostEstimate(
            flops=2 * n * rows * kin * cols, bytes_accessed=4 * n * rows * half + 2 * kin * cols, transcendentals=0
        ),
    )(*lows, *highs, basis, *before)


def place(blk, ring, me, counts, slots, *refs):
    *hops, hot = refs
    cap = slots.shape[1]
    owners = CHIPS * CORES
    stripe, per = blk * owners, ring // owners
    own = me[0]
    z, c = own // CORES, own % CORES
    start = jnp.int32(0)
    for o in range(owners):
        start += jnp.where(o < own, counts[o], 0)
    slot = lax.broadcasted_iota(I32, (1, cap), 1)
    spot = lax.rem(start + slot, jnp.int32(ring))
    goal = lax.div(lax.rem(spot, jnp.int32(stripe)), jnp.int32(blk))
    hop = ((goal // CORES - z + CHIPS) & (CHIPS - 1)) * CORES + ((goal & 1) ^ c)
    row = hop * per + lax.div(spot, jnp.int32(stripe)) * blk + lax.rem(spot, jnp.int32(blk))
    row = jnp.where(slot < counts[own], row, -1)
    for r in range(0, ring, per):
        here = lax.broadcasted_iota(I32, (per, cap), 0) + r == row
        hot[r : r + per] = here.astype(F32).astype(BF16)
    laid = lax.dot_general(hot[...], slots[...], (((1,), (1,)), ((), ())), preferred_element_type=F32).astype(BF16)
    for r in range(0, ring, per):
        hops[r // per // CORES][r // per % CORES] = laid[r : r + per]


def placed(basis_slots, col_counts, img, own, groups, blk, ring):
    kin, cap = basis_slots.shape
    depth = kin // groups
    piece = lax.dynamic_slice(basis_slots, (img * depth, jnp.int32(0)), (depth, cap))
    scalars, inside = pl.BlockSpec(memory_space=pltpu.SMEM), pl.BlockSpec(memory_space=pltpu.VMEM)
    return pl.pallas_call(
        functools.partial(place, blk, ring),
        out_shape=[jax.ShapeDtypeStruct((CORES, ring // CHIPS // CORES, depth), BF16)] * CHIPS,
        in_specs=[scalars, scalars, inside],
        out_specs=[inside] * CHIPS,
        scratch_shapes=[pltpu.VMEM((ring, cap), BF16)],
        compiler_params=pltpu.CompilerParams(vmem_limit_bytes=28 << 20),
        cost_estimate=pl.CostEstimate(flops=2 * ring * cap * depth, bytes_accessed=4 * depth * cap, transcendentals=0),
    )(own.astype(I32).reshape(1), col_counts, piece)


def collect(blk, ring, wide, me, counts, *refs):
    kept, given, out = refs[:CHIPS], refs[CHIPS : 2 * CHIPS], refs[-1]
    owners = CHIPS * CORES
    stripe, per = blk * owners, ring // owners
    own = me[0]
    z, c = own // CORES, own % CORES
    spot = lax.broadcasted_iota(I32, (per, 1), 0)
    at = lax.div(spot, jnp.int32(blk)) * stripe + own * blk + lax.rem(spot, jnp.int32(blk))
    column = lax.broadcasted_iota(I32, (per, out.shape[1]), 1)
    total = jnp.zeros(out.shape, F32)
    for hop in range(CHIPS):
        for other in range(CORES):
            source = ((z - hop + CHIPS) & (CHIPS - 1)) * CORES + (c ^ other)
            begin = jnp.int32(0)
            for o in range(owners):
                begin += jnp.where(o < source, counts[o], 0)
            offset = lax.rem(at - begin + owners * ring, jnp.int32(ring))
            index = begin + offset
            target = lax.div(index, jnp.int32(stripe)) * wide + lax.rem(index, jnp.int32(blk))
            target = jnp.where(offset < counts[source], target, -1)
            keep = (column == target).astype(F32).astype(BF16)
            piece = given[hop][...] if other else kept[hop][0]
            total += jnp.dot(piece.T, keep, preferred_element_type=F32)
    out[...] = total.astype(BF16)


def collected(hops, given, col_counts, own, groups, blk, ring, wide):
    per, depth = given[0].shape
    scalars, inside = pl.BlockSpec(memory_space=pltpu.SMEM), pl.BlockSpec(memory_space=pltpu.VMEM)
    return pl.pallas_call(
        functools.partial(collect, blk, ring, wide),
        out_shape=jax.ShapeDtypeStruct((depth, groups * wide), BF16),
        in_specs=[scalars, scalars] + [inside] * (2 * CHIPS),
        out_specs=inside,
        compiler_params=pltpu.CompilerParams(vmem_limit_bytes=28 << 20),
        cost_estimate=pl.CostEstimate(
            flops=2 * ring * depth * groups * wide, bytes_accessed=4 * depth * groups * wide, transcendentals=0
        ),
    )(own.astype(I32).reshape(1), col_counts, *hops, *given)


def up(a, step):
    pairs = [(z * CORES + c, (z + step) % CHIPS * CORES + c) for z in range(CHIPS) for c in range(CORES)]
    return lax.ppermute(a, "own", pairs)


def swap(a):
    return lax.ppermute(a, "own", [(o, o ^ 1) for o in range(CHIPS * CORES)])


def balanced_basis(basis_slots, col_counts, img, own, groups, blk, wide, first):
    owners = CHIPS * CORES
    kin, cap = basis_slots.shape
    stripe = blk * owners
    ring = -(-cap // stripe) * stripe
    hops = placed(basis_slots, col_counts, img, own, groups, blk, ring)
    hops = [hops[0], up(hops[1], 1), up(hops[2], 2), up(hops[3], -1)]
    given = [swap(hop[1]) for hop in hops]
    hops, given, first = lax.optimization_barrier((hops, given, first))
    mine = collected(hops, given, col_counts, own, groups, blk, ring, wide)
    return lax.all_gather(mine, "img", axis=0, tiled=True), first


def gathered(low, high):
    low_down, high_up = up(low, 1), up(high, -1)
    mine = (low, high, swap(low), swap(high))
    low, high, low_down, high_up, mine = lax.optimization_barrier((low, high, low_down, high_up, mine))
    high_down, low_up = up(high, 1), up(low, -1)
    other_low, other_high = swap(low_down), swap(high_up)
    low_down, high_up, high_down, low_up, other_low, other_high = lax.optimization_barrier(
        (low_down, high_up, high_down, low_up, other_low, other_high)
    )
    far = (up(low_down, 1), up(high_up, -1))
    pairs = [mine[:2], mine[2:], (low_down, high_down), (other_low, swap(high_down)), (low_up, high_up)]
    return pairs + [(swap(low_up), other_high)], far


def shards(patches, grads, basis_g, basis_slots, col_counts):
    groups = lax.axis_size("img")
    owners = CHIPS * CORES
    img, own = lax.axis_index("img"), lax.axis_index("own")
    rows, kin = patches.shape
    gout = basis_g.shape[1]
    blk = kin // (groups * owners)
    proj = jnp.dot(grads, basis_g, preferred_element_type=F32).astype(BF16)
    half = (kin + gout) // 2
    low, high = patches[:, :half], jnp.concatenate([patches[:, half:], proj], axis=1)
    wide = -(-(blk + 1) // 8) * 8
    basis, (low, high) = balanced_basis(basis_slots, col_counts, img, own, groups, blk, wide, (low, high))
    near, far = gathered(low, high)
    sums = added("near", near, basis)
    far, sums = lax.optimization_barrier((far, sums))
    partner = swap(far[0]), swap(far[1])
    more = added("far", [far], basis)
    total = added("last", [partner], basis, more, sums, block=(blk, wide))
    parts = lax.all_to_all(total.astype(jnp.float16).reshape(groups, wide, gout), "img", 0, 0, tiled=True)
    level = parts[:, blk : blk + 1, :1].astype(F32) - TOP
    return jnp.sum(parts[:, :blk].astype(F32) * jnp.exp2(level), axis=0) / F32(owners * rows // POS * groups)


def solution(mesh):
    in_specs = (P(("img", "own"), None), P(("img", "own"), None), P(), P(None, "own"), P())
    out_specs = P(("img", "own"), None)
    return jax.shard_map(shards, mesh=mesh, in_specs=in_specs, out_specs=out_specs, check_vma=False)
```

```python
import functools

import jax
import jax.numpy as jnp
from jax import lax
from jax.experimental import pallas as pl
from jax.experimental.pallas import tpu as pltpu
from jax.sharding import PartitionSpec as P

POS = 49
CHIPS = 4
CORES = 2
TOP = 13.0
LIMITS = {"near": 54, "far": 28, "last": 28}
F32, BF16, I32 = jnp.float32, jnp.bfloat16, jnp.int32


def accumulate(n, chunk, mode, block, *refs):
    lows, highs = refs[:n], refs[n : 2 * n]
    staged = mode == "near"
    before = []
    if staged:
        basis, total, flip, low, high, low_sems, high_sems = refs[2 * n :]
    elif mode == "far":
        basis, total, flip = refs[2 * n :]
    else:
        basis, *before, out, flip, total = refs[2 * n :]
    rows, half = lows[0].shape
    kin, cols = basis.shape
    rest = kin - half
    gout = half - rest
    if staged:
        lefts = [pltpu.make_async_copy(lows[k], low.at[k % 2], low_sems.at[k % 2]) for k in range(n)]
        rights = [pltpu.make_async_copy(highs[k], high.at[k % 2], high_sems.at[k % 2]) for k in range(n)]
        lows, highs = [low.at[k % 2] for k in range(n)], [high.at[k % 2] for k in range(n)]
        lefts[0].start()
        rights[0].start()
    image = lax.broadcasted_iota(I32, (rows, gout), 0) // POS
    for k in range(n):
        if staged:
            lefts[k].wait()
            if k + 1 < n:
                lefts[k + 1].start()
        proj = jnp.dot(lows[k][...], basis[:half], preferred_element_type=F32)
        if staged:
            rights[k].wait()
            if k + 1 < n:
                rights[k + 1].start()
        proj += jnp.dot(highs[k][:, :rest], basis[half:], preferred_element_type=F32)
        flip[k % 2] = proj.astype(BF16).T
        grads = highs[k][:, rest:]
        apart = [jnp.where(image == m, grads, jnp.zeros_like(grads)) for m in range(rows // POS)]
        sources = [total] if k else before
        for s in range(0, cols, chunk):
            left = flip[k % 2, s : s + chunk]
            squares = jnp.zeros((chunk, gout), F32)
            for source in sources:
                squares += source[s : s + chunk]
            for one in apart:
                coef = jnp.dot(left, one, preferred_element_type=F32)
                squares += coef * coef
            total[s : s + chunk] = squares
    if block:
        peak = jnp.max(jnp.max(total[...], axis=0, keepdims=True), axis=1, keepdims=True)
        level = jnp.floor(jnp.log(jnp.maximum(peak, 1e-30)) * 1.4426950408889634)
        row = lax.rem(lax.broadcasted_iota(I32, (cols, gout), 0), jnp.int32(block[1]))
        out[...] = jnp.where(row == block[0], level, total[...] * jnp.exp2(TOP - level))


def added(mode, pairs, basis, *before, block=()):
    n = len(pairs)
    lows, highs = zip(*pairs)
    rows, half = lows[0].shape
    kin, cols = basis.shape
    gout = 2 * half - kin
    inside, outside = pl.BlockSpec(memory_space=pltpu.VMEM), pl.BlockSpec(memory_space=pltpu.HBM)
    room = [pltpu.VMEM((2, cols, rows), BF16)]
    if mode == "near":
        pair, sems = pltpu.VMEM((2, rows, half), BF16), pltpu.SemaphoreType.DMA
        room += [pair, pair, sems((2,)), sems((2,))]
    elif mode == "last":
        room += [pltpu.VMEM((cols, gout), F32)]
    return pl.pallas_call(
        functools.partial(accumulate, n, cols // 2, mode, block),
        out_shape=jax.ShapeDtypeStruct((cols, gout), F32),
        in_specs=[outside if mode == "near" else inside] * (2 * n) + [inside] * (1 + len(before)),
        out_specs=inside,
        scratch_shapes=room,
        compiler_params=pltpu.CompilerParams(vmem_limit_bytes=LIMITS[mode] << 20),
        cost_estimate=pl.CostEstimate(
            flops=2 * n * rows * kin * cols, bytes_accessed=4 * n * rows * half + 2 * kin * cols, transcendentals=0
        ),
    )(*lows, *highs, basis, *before)


def place(blk, ring, me, counts, slots, *refs):
    *hops, hot = refs
    cap = slots.shape[1]
    owners = CHIPS * CORES
    stripe, per = blk * owners, ring // owners
    own = me[0]
    z, c = own // CORES, own % CORES
    start = jnp.int32(0)
    for o in range(owners):
        start += jnp.where(o < own, counts[o], 0)
    slot = lax.broadcasted_iota(I32, (1, cap), 1)
    spot = lax.rem(start + slot, jnp.int32(ring))
    goal = lax.div(lax.rem(spot, jnp.int32(stripe)), jnp.int32(blk))
    hop = ((goal // CORES - z + CHIPS) & (CHIPS - 1)) * CORES + ((goal & 1) ^ c)
    row = hop * per + lax.div(spot, jnp.int32(stripe)) * blk + lax.rem(spot, jnp.int32(blk))
    row = jnp.where(slot < counts[own], row, -1)
    for r in range(0, ring, per):
        here = lax.broadcasted_iota(I32, (per, cap), 0) + r == row
        hot[r : r + per] = here.astype(F32).astype(BF16)
    laid = lax.dot_general(hot[...], slots[...], (((1,), (1,)), ((), ())), preferred_element_type=F32).astype(BF16)
    for r in range(0, ring, per):
        hops[r // per // CORES][r // per % CORES] = laid[r : r + per]


def placed(basis_slots, col_counts, img, own, groups, blk, ring):
    kin, cap = basis_slots.shape
    depth = kin // groups
    piece = lax.dynamic_slice(basis_slots, (img * depth, jnp.int32(0)), (depth, cap))
    scalars, inside = pl.BlockSpec(memory_space=pltpu.SMEM), pl.BlockSpec(memory_space=pltpu.VMEM)
    return pl.pallas_call(
        functools.partial(place, blk, ring),
        out_shape=[jax.ShapeDtypeStruct((CORES, ring // CHIPS // CORES, depth), BF16)] * CHIPS,
        in_specs=[scalars, scalars, inside],
        out_specs=[inside] * CHIPS,
        scratch_shapes=[pltpu.VMEM((ring, cap), BF16)],
        compiler_params=pltpu.CompilerParams(vmem_limit_bytes=28 << 20),
        cost_estimate=pl.CostEstimate(flops=2 * ring * cap * depth, bytes_accessed=4 * depth * cap, transcendentals=0),
    )(own.astype(I32).reshape(1), col_counts, piece)


def collect(blk, ring, wide, me, counts, *refs):
    kept, given, out = refs[:CHIPS], refs[CHIPS : 2 * CHIPS], refs[-1]
    owners = CHIPS * CORES
    stripe, per = blk * owners, ring // owners
    own = me[0]
    z, c = own // CORES, own % CORES
    spot = lax.broadcasted_iota(I32, (per, 1), 0)
    at = lax.div(spot, jnp.int32(blk)) * stripe + own * blk + lax.rem(spot, jnp.int32(blk))
    column = lax.broadcasted_iota(I32, (per, out.shape[1]), 1)
    total = jnp.zeros(out.shape, F32)
    for hop in range(CHIPS):
        for other in range(CORES):
            source = ((z - hop + CHIPS) & (CHIPS - 1)) * CORES + (c ^ other)
            begin = jnp.int32(0)
            for o in range(owners):
                begin += jnp.where(o < source, counts[o], 0)
            offset = lax.rem(at - begin + owners * ring, jnp.int32(ring))
            index = begin + offset
            target = lax.div(index, jnp.int32(stripe)) * wide + lax.rem(index, jnp.int32(blk))
            target = jnp.where(offset < counts[source], target, -1)
            keep = (column == target).astype(F32).astype(BF16)
            piece = given[hop][...] if other else kept[hop][0]
            total += jnp.dot(piece.T, keep, preferred_element_type=F32)
    out[...] = total.astype(BF16)


def collected(hops, given, col_counts, own, groups, blk, ring, wide):
    per, depth = given[0].shape
    scalars, inside = pl.BlockSpec(memory_space=pltpu.SMEM), pl.BlockSpec(memory_space=pltpu.VMEM)
    return pl.pallas_call(
        functools.partial(collect, blk, ring, wide),
        out_shape=jax.ShapeDtypeStruct((depth, groups * wide), BF16),
        in_specs=[scalars, scalars] + [inside] * (2 * CHIPS),
        out_specs=inside,
        compiler_params=pltpu.CompilerParams(vmem_limit_bytes=28 << 20),
        cost_estimate=pl.CostEstimate(
            flops=2 * ring * depth * groups * wide, bytes_accessed=4 * depth * groups * wide, transcendentals=0
        ),
    )(own.astype(I32).reshape(1), col_counts, *hops, *given)


def up(a, step):
    pairs = [(z * CORES + c, (z + step) % CHIPS * CORES + c) for z in range(CHIPS) for c in range(CORES)]
    return lax.ppermute(a, "own", pairs)


def swap(a):
    return lax.ppermute(a, "own", [(o, o ^ 1) for o in range(CHIPS * CORES)])


def balanced_basis(basis_slots, col_counts, img, own, groups, blk, wide, first):
    owners = CHIPS * CORES
    kin, cap = basis_slots.shape
    stripe = blk * owners
    ring = -(-cap // stripe) * stripe
    hops = placed(basis_slots, col_counts, img, own, groups, blk, ring)
    hops = [hops[0], up(hops[1], 1), up(hops[2], 2), up(hops[3], -1)]
    given = [swap(hop[1]) for hop in hops]
    hops, given, first = lax.optimization_barrier((hops, given, first))
    mine = collected(hops, given, col_counts, own, groups, blk, ring, wide)
    return lax.all_gather(mine, "img", axis=0, tiled=True), first


def gathered(low, high):
    low_down, high_up = up(low, 1), up(high, -1)
    mine = (low, high, swap(low), swap(high))
    low, high, low_down, high_up, mine = lax.optimization_barrier((low, high, low_down, high_up, mine))
    high_down, low_up = up(high, 1), up(low, -1)
    other_low, other_high = swap(low_down), swap(high_up)
    low_down, high_up, high_down, low_up, other_low, other_high = lax.optimization_barrier(
        (low_down, high_up, high_down, low_up, other_low, other_high)
    )
    far = (up(low_down, 1), up(high_up, -1))
    pairs = [mine[:2], mine[2:], (low_down, high_down), (other_low, swap(high_down)), (low_up, high_up)]
    return pairs + [(swap(low_up), other_high)], far


def shards(patches, grads, basis_g, basis_slots, col_counts):
    groups = lax.axis_size("img")
    owners = CHIPS * CORES
    img, own = lax.axis_index("img"), lax.axis_index("own")
    rows, kin = patches.shape
    gout = basis_g.shape[1]
    blk = kin // (groups * owners)
    proj = jnp.dot(grads, basis_g, preferred_element_type=F32).astype(BF16)
    half = (kin + gout) // 2
    low, high = patches[:, :half], jnp.concatenate([patches[:, half:], proj], axis=1)
    wide = -(-(blk + 1) // 8) * 8
    basis, (low, high) = balanced_basis(basis_slots, col_counts, img, own, groups, blk, wide, (low, high))
    near, far = gathered(low, high)
    sums = added("near", near, basis)
    far, sums = lax.optimization_barrier((far, sums))
    partner = swap(far[0]), swap(far[1])
    more = added("far", [far], basis)
    total = added("last", [partner], basis, more, sums, block=(blk, wide))
    parts = lax.all_to_all(total.astype(jnp.float16).reshape(groups, wide, gout), "img", 0, 0, tiled=True)
    level = parts[:, blk : blk + 1, :1].astype(F32) - TOP
    return jnp.sum(parts[:, :blk].astype(F32) * jnp.exp2(level), axis=0) / F32(owners * rows // POS * groups)


def solution(mesh):
    in_specs = (P(("img", "own"), None), P(("img", "own"), None), P(), P(None, "own"), P())
    out_specs = P(("img", "own"), None)
    return jax.shard_map(shards, mesh=mesh, in_specs=in_specs, out_specs=out_specs, check_vma=False)
```

```python
import functools

import jax
import jax.numpy as jnp
from jax import lax
from jax.experimental import pallas as pl
from jax.experimental.pallas import tpu as pltpu
from jax.sharding import PartitionSpec as P

POS = 49
CHIPS = 4
CORES = 2
TOP = 13.0
LIMITS = {"near": 54, "far": 28, "last": 28}
F32, BF16, I32 = jnp.float32, jnp.bfloat16, jnp.int32


def accumulate(n, chunk, mode, block, *refs):
    lows, highs = refs[:n], refs[n : 2 * n]
    staged = mode == "near"
    before = []
    if staged:
        basis, total, flip, held, basis_sems, low, high, low_sems, high_sems = refs[2 * n :]
    elif mode == "far":
        basis, total, flip = refs[2 * n :]
    else:
        basis, *before, out, flip, total = refs[2 * n :]
    rows, half = lows[0].shape
    kin, cols = basis.shape
    rest = kin - half
    gout = half - rest
    parts = 2
    if staged:
        lefts = [pltpu.make_async_copy(lows[k], low.at[k % 2], low_sems.at[k % 2]) for k in range(n)]
        rights = [pltpu.make_async_copy(highs[k], high.at[k % 2], high_sems.at[k % 2]) for k in range(n)]
        lows, highs = [low.at[k % 2] for k in range(n)], [high.at[k % 2] for k in range(n)]
        lefts[0].start()
        edges = [half * i // parts for i in range(parts)] + [half + rest * i // parts for i in range(parts + 1)]
        spans = [pl.ds(a, b - a) for a, b in zip(edges, edges[1:])]
        pieces = [pltpu.make_async_copy(basis.at[s], held.at[s], basis_sems.at[i]) for i, s in enumerate(spans)]
        for i, piece in enumerate(pieces):
            if i == parts:
                rights[0].start()
            piece.start()
        basis = held
    image = lax.broadcasted_iota(I32, (rows, gout), 0) // POS
    for k in range(n):
        if staged:
            lefts[k].wait()
            if 0 < k < n - 1:
                lefts[k + 1].start()
        if staged and k == 0:
            proj = jnp.zeros((rows, cols), F32)
            for i in range(2 * parts):
                if i == parts:
                    rights[0].wait()
                    lefts[1].start()
                pieces[i].wait()
                if i == 2 * parts - 1:
                    rights[1].start()
                a, b = edges[i], edges[i + 1]
                left = lows[0][:, a:b] if i < parts else highs[0][:, a - half : b - half]
                proj += jnp.dot(left, basis[a:b], preferred_element_type=F32)
        else:
            proj = jnp.dot(lows[k][...], basis[:half], preferred_element_type=F32)
            if staged:
                rights[k].wait()
                if k + 1 < n:
                    rights[k + 1].start()
            proj += jnp.dot(highs[k][:, :rest], basis[half:], preferred_element_type=F32)
        flip[k % 2] = proj.astype(BF16).T
        grads = highs[k][:, rest:]
        apart = [jnp.where(image == m, grads, jnp.zeros_like(grads)) for m in range(rows // POS)]
        sources = [total] if k else before
        for s in range(0, cols, chunk):
            left = flip[k % 2, s : s + chunk]
            squares = jnp.zeros((chunk, gout), F32)
            for source in sources:
                squares += source[s : s + chunk]
            for one in apart:
                coef = jnp.dot(left, one, preferred_element_type=F32)
                squares += coef * coef
            total[s : s + chunk] = squares
    if block:
        peak = jnp.max(jnp.max(total[...], axis=0, keepdims=True), axis=1, keepdims=True)
        level = jnp.floor(jnp.log(jnp.maximum(peak, 1e-30)) * 1.4426950408889634)
        row = lax.rem(lax.broadcasted_iota(I32, (cols, gout), 0), jnp.int32(block[1]))
        out[...] = jnp.where(row == block[0], level, total[...] * jnp.exp2(TOP - level))


def added(mode, pairs, basis, *before, block=()):
    n = len(pairs)
    lows, highs = zip(*pairs)
    rows, half = lows[0].shape
    kin, cols = basis.shape
    gout = 2 * half - kin
    inside, outside = pl.BlockSpec(memory_space=pltpu.VMEM), pl.BlockSpec(memory_space=pltpu.HBM)
    room = [pltpu.VMEM((2, cols, rows), BF16)]
    if mode == "near":
        pair, sems = pltpu.VMEM((2, rows, half), BF16), pltpu.SemaphoreType.DMA
        room += [pltpu.VMEM((kin, cols), BF16), sems((4,)), pair, pair, sems((2,)), sems((2,))]
    elif mode == "last":
        room += [pltpu.VMEM((cols, gout), F32)]
    return pl.pallas_call(
        functools.partial(accumulate, n, cols // 2, mode, block),
        out_shape=jax.ShapeDtypeStruct((cols, gout), F32),
        in_specs=[outside if mode == "near" else inside] * (2 * n + 1) + [inside] * len(before),
        out_specs=inside,
        scratch_shapes=room,
        compiler_params=pltpu.CompilerParams(vmem_limit_bytes=LIMITS[mode] << 20),
        cost_estimate=pl.CostEstimate(
            flops=2 * n * rows * kin * cols, bytes_accessed=4 * n * rows * half + 2 * kin * cols, transcendentals=0
        ),
    )(*lows, *highs, basis, *before)


def place(blk, ring, me, counts, slots, *refs):
    *hops, hot = refs
    cap = slots.shape[1]
    owners = CHIPS * CORES
    stripe, per = blk * owners, ring // owners
    own = me[0]
    z, c = own // CORES, own % CORES
    start = jnp.int32(0)
    for o in range(owners):
        start += jnp.where(o < own, counts[o], 0)
    slot = lax.broadcasted_iota(I32, (1, cap), 1)
    spot = lax.rem(start + slot, jnp.int32(ring))
    goal = lax.div(lax.rem(spot, jnp.int32(stripe)), jnp.int32(blk))
    hop = ((goal // CORES - z + CHIPS) & (CHIPS - 1)) * CORES + ((goal & 1) ^ c)
    row = hop * per + lax.div(spot, jnp.int32(stripe)) * blk + lax.rem(spot, jnp.int32(blk))
    row = jnp.where(slot < counts[own], row, -1)
    for r in range(0, ring, per):
        here = lax.broadcasted_iota(I32, (per, cap), 0) + r == row
        hot[r : r + per] = here.astype(F32).astype(BF16)
    laid = lax.dot_general(hot[...], slots[...], (((1,), (1,)), ((), ())), preferred_element_type=F32).astype(BF16)
    for r in range(0, ring, per):
        hops[r // per // CORES][r // per % CORES] = laid[r : r + per]


def placed(basis_slots, col_counts, img, own, groups, blk, ring):
    kin, cap = basis_slots.shape
    depth = kin // groups
    piece = lax.dynamic_slice(basis_slots, (img * depth, jnp.int32(0)), (depth, cap))
    scalars, inside = pl.BlockSpec(memory_space=pltpu.SMEM), pl.BlockSpec(memory_space=pltpu.VMEM)
    return pl.pallas_call(
        functools.partial(place, blk, ring),
        out_shape=[jax.ShapeDtypeStruct((CORES, ring // CHIPS // CORES, depth), BF16)] * CHIPS,
        in_specs=[scalars, scalars, inside],
        out_specs=[inside] * CHIPS,
        scratch_shapes=[pltpu.VMEM((ring, cap), BF16)],
        compiler_params=pltpu.CompilerParams(vmem_limit_bytes=28 << 20),
        cost_estimate=pl.CostEstimate(flops=2 * ring * cap * depth, bytes_accessed=4 * depth * cap, transcendentals=0),
    )(own.astype(I32).reshape(1), col_counts, piece)


def collect(blk, ring, wide, me, counts, *refs):
    kept, given, out = refs[:CHIPS], refs[CHIPS : 2 * CHIPS], refs[-1]
    owners = CHIPS * CORES
    stripe, per = blk * owners, ring // owners
    own = me[0]
    z, c = own // CORES, own % CORES
    spot = lax.broadcasted_iota(I32, (per, 1), 0)
    at = lax.div(spot, jnp.int32(blk)) * stripe + own * blk + lax.rem(spot, jnp.int32(blk))
    column = lax.broadcasted_iota(I32, (per, out.shape[1]), 1)
    total = jnp.zeros(out.shape, F32)
    for hop in range(CHIPS):
        for other in range(CORES):
            source = ((z - hop + CHIPS) & (CHIPS - 1)) * CORES + (c ^ other)
            begin = jnp.int32(0)
            for o in range(owners):
                begin += jnp.where(o < source, counts[o], 0)
            offset = lax.rem(at - begin + owners * ring, jnp.int32(ring))
            index = begin + offset
            target = lax.div(index, jnp.int32(stripe)) * wide + lax.rem(index, jnp.int32(blk))
            target = jnp.where(offset < counts[source], target, -1)
            keep = (column == target).astype(F32).astype(BF16)
            piece = given[hop][...] if other else kept[hop][0]
            total += jnp.dot(piece.T, keep, preferred_element_type=F32)
    out[...] = total.astype(BF16)


def collected(hops, given, col_counts, own, groups, blk, ring, wide):
    per, depth = given[0].shape
    scalars, inside = pl.BlockSpec(memory_space=pltpu.SMEM), pl.BlockSpec(memory_space=pltpu.VMEM)
    return pl.pallas_call(
        functools.partial(collect, blk, ring, wide),
        out_shape=jax.ShapeDtypeStruct((depth, groups * wide), BF16),
        in_specs=[scalars, scalars] + [inside] * (2 * CHIPS),
        out_specs=inside,
        compiler_params=pltpu.CompilerParams(vmem_limit_bytes=28 << 20),
        cost_estimate=pl.CostEstimate(
            flops=2 * ring * depth * groups * wide, bytes_accessed=4 * depth * groups * wide, transcendentals=0
        ),
    )(own.astype(I32).reshape(1), col_counts, *hops, *given)


def up(a, step):
    pairs = [(z * CORES + c, (z + step) % CHIPS * CORES + c) for z in range(CHIPS) for c in range(CORES)]
    return lax.ppermute(a, "own", pairs)


def swap(a):
    return lax.ppermute(a, "own", [(o, o ^ 1) for o in range(CHIPS * CORES)])


def balanced_basis(basis_slots, col_counts, img, own, groups, blk, wide, first):
    owners = CHIPS * CORES
    kin, cap = basis_slots.shape
    stripe = blk * owners
    ring = -(-cap // stripe) * stripe
    hops = placed(basis_slots, col_counts, img, own, groups, blk, ring)
    hops = [hops[0], up(hops[1], 1), up(hops[2], 2), up(hops[3], -1)]
    given = [swap(hop[1]) for hop in hops]
    hops, given, first = lax.optimization_barrier((hops, given, first))
    mine = collected(hops, given, col_counts, own, groups, blk, ring, wide)
    return lax.all_gather(mine, "img", axis=0, tiled=True), first


def gathered(low, high):
    low_down, high_up = up(low, 1), up(high, -1)
    mine = (low, high, swap(low), swap(high))
    low, high, low_down, high_up, mine = lax.optimization_barrier((low, high, low_down, high_up, mine))
    high_down, low_up = up(high, 1), up(low, -1)
    other_low, other_high = swap(low_down), swap(high_up)
    low_down, high_up, high_down, low_up, other_low, other_high = lax.optimization_barrier(
        (low_down, high_up, high_down, low_up, other_low, other_high)
    )
    far = (up(low_down, 1), up(high_up, -1))
    pairs = [mine[:2], mine[2:], (low_down, high_down), (other_low, swap(high_down)), (low_up, high_up)]
    return pairs + [(swap(low_up), other_high)], far


def shards(patches, grads, basis_g, basis_slots, col_counts):
    groups = lax.axis_size("img")
    owners = CHIPS * CORES
    img, own = lax.axis_index("img"), lax.axis_index("own")
    rows, kin = patches.shape
    gout = basis_g.shape[1]
    blk = kin // (groups * owners)
    proj = jnp.dot(grads, basis_g, preferred_element_type=F32).astype(BF16)
    half = (kin + gout) // 2
    low, high = patches[:, :half], jnp.concatenate([patches[:, half:], proj], axis=1)
    wide = -(-(blk + 1) // 8) * 8
    basis, (low, high) = balanced_basis(basis_slots, col_counts, img, own, groups, blk, wide, (low, high))
    near, far = gathered(low, high)
    sums = added("near", near, basis)
    far, sums = lax.optimization_barrier((far, sums))
    partner = swap(far[0]), swap(far[1])
    more = added("far", [far], basis)
    total = added("last", [partner], basis, more, sums, block=(blk, wide))
    parts = lax.all_to_all(total.astype(jnp.float16).reshape(groups, wide, gout), "img", 0, 0, tiled=True)
    level = parts[:, blk : blk + 1, :1].astype(F32) - TOP
    return jnp.sum(parts[:, :blk].astype(F32) * jnp.exp2(level), axis=0) / F32(owners * rows // POS * groups)


def solution(mesh):
    in_specs = (P(("img", "own"), None), P(("img", "own"), None), P(), P(None, "own"), P())
    out_specs = P(("img", "own"), None)
    return jax.shard_map(shards, mesh=mesh, in_specs=in_specs, out_specs=out_specs, check_vma=False)
```
